256 devices in a mesh: ctx: 64 (over x_lo, z, y), batch: 4 (over x_hi, core).
Axes of the slice: x: 4 (x_hi: 2, x_lo: 2; x = x_hi * 2 + x_lo), y: 4, z: 8, core: 2. Of those that a mesh axis runs over, the one named last changes fastest.
Arguments:
- queries: bfloat16 [49152, 1024], P(('batch', 'ctx')), parts along dimension 0, may hold values from -40 to 40
- keys: bfloat16 [49152, 128], P(('batch', 'ctx')), parts along dimension 0, may hold values from -4.5 to 4.5
- values: bfloat16 [49152, 128], P(('batch', 'ctx')), parts along dimension 0, may hold values from -6 to 6
- steal_block: int32 [32], replicated, may hold values from 0 to 1
Outputs:
- attended: bfloat16 [49152, 1024], P(('batch', 'ctx')), parts along dimension 0
The draws below stay inside these ranges and needn't reach their ends.
There are 4 independent parts, one for each index of `batch`. The reference program is written for one: setup_inputs(seed, part) draws one part's arguments, and reference() takes and returns one part's arrays. A program takes and returns all parts, laid end to end along the dimension named above; an argument that names none is the same for every part. Nothing has to cross between parts.
All inputs are finite; a program needn't handle non-finite values.
Results may differ from the reference program's by a relative error of at most 0.0055.
Values may be sent and summed in bfloat16 or wider, within the bound.
No kernel may reach another device: no remote copies, remote signals or barrier semaphores. Data moves between devices by JAX's collectives and lax.ppermute only.
A program may use at most 64 MiB of HBM per device.

```python
import math
import jax
import jax.numpy as jnp
from jax import lax

H = 8
DH = 128
TOK_DEV = 192
TOKENS = 12288
PAIRS = 32
N_CTX = 64


def shared_draws(key):
    gauss = jax.random.truncated_normal(jax.random.fold_in(key, 101), -4.5, 4.5, (TOKENS, DH), jnp.float32)
    return gauss


def draw_keys(key, part):
    gauss = shared_draws(key)
    drawn = gauss
    return drawn.astype(jnp.bfloat16)


def draw_queries(key, part):
    key = jax.random.fold_in(key, 7)
    drawn = 2.5 * jax.random.truncated_normal(key, -4.5, 4.5, (TOKENS, H * DH), jnp.float32)
    return drawn.astype(jnp.bfloat16)


def place_ends(values, rng, least, largest):
    longest = values.shape.index(max(values.shape))
    spots = []
    for shift in (0, 1):
        where = [jax.random.randint(jax.random.fold_in(rng, axis), (), 0, length) for axis, length in enumerate(values.shape)]
        where[longest] = (where[longest] + shift) % values.shape[longest]
        spots.append(tuple(where))
    return values.at[spots[0]].set(least).at[spots[1]].set(largest)


def shard_levels(stream_key, dims, cuts, least, largest):
    gain, own = 1.0, jax.random.fold_in(stream_key, 6)
    for position, shards_of in cuts:
        heights = jnp.exp(jax.random.uniform(jax.random.fold_in(own, position), (shards_of,), jnp.float32, least / len(cuts), largest / len(cuts)))
        gain = gain * jnp.repeat(heights, dims[position] // shards_of).reshape([-1 if axis == position else 1 for axis in range(len(dims))])
    return gain


def centred(own_key, extent, width, bound, split=(), kind=jnp.bfloat16):
    entries = jax.random.normal(own_key, extent, jnp.float32) * width
    if len(split) > 0:
        entries = shard_levels(own_key, extent, split, -0.22, 0.18) * entries
    return jnp.clip(entries, min=-bound, max=bound).astype(kind)


def setup_inputs(seed: int = 0, part: int = 0) -> dict:
    arg_keys = jax.random.split(jax.random.key(seed), 5)
    part_splits = jax.random.split(jax.random.fold_in(arg_keys[4], part), 5)
    queries = draw_queries(jax.random.fold_in(jax.random.fold_in(arg_keys[4], part), 71), part)
    keys = draw_keys(jax.random.fold_in(jax.random.fold_in(arg_keys[4], part), 71), part)
    values = centred(part_splits[2], (TOKENS, DH), 1.0, 6.0, ((0, 64),))
    steal_block = place_ends(jax.random.randint(arg_keys[3], (PAIRS,), 0, 2), jax.random.fold_in(arg_keys[3], 1), 0, 1).astype(jnp.int32)
    return {"queries": queries, "keys": keys, "values": values, "steal_block": steal_block}


floor_score = -1e+30

def reference(queries, keys, values, steal_block):
    total_rows = queries.shape[0]
    head_width = keys.shape[1]
    head_count = queries.shape[1] // head_width
    block_rows = TOK_DEV // 2
    block_count = total_rows // block_rows
    query_blocks = queries.reshape(block_count, block_rows, head_count, head_width)
    key_index = jnp.arange(total_rows, dtype=jnp.int32)
    keys_wide = keys.astype(jnp.float32)
    values_wide = values.astype(jnp.float32)

    def score_block(inputs):
        query_tile, block_index = inputs
        positions = block_index * block_rows + jnp.arange(block_rows, dtype=jnp.int32)
        scores = jnp.einsum('rhd,td->rht', query_tile.astype(jnp.float32), keys_wide) * (1.0 / math.sqrt(head_width))
        allowed = key_index[None, None, :] <= positions[:, None, None]
        scores = jnp.where(allowed, scores, floor_score)
        row_max = lax.optimization_barrier(jnp.max(scores, axis=2, keepdims=True))
        weights = jnp.where(allowed, jnp.exp(scores - row_max), 0.0)
        row_total = lax.optimization_barrier(jnp.sum(weights, axis=2))
        rounded = lax.optimization_barrier(weights.astype(jnp.bfloat16)).astype(jnp.float32)
        context = jnp.einsum('rht,td->rhd', rounded, values_wide) / row_total[:, :, None]
        return context.astype(jnp.bfloat16).reshape(block_rows, head_count * head_width)
    context = lax.map(score_block, (query_blocks, jnp.arange(block_count, dtype=jnp.int32)))
    block_ids = jnp.arange(block_count, dtype=jnp.int32)
    owner = block_ids // 2
    half_index = block_ids % 2
    mirror = N_CTX - 1 - owner
    traded = steal_block[jnp.minimum(owner, mirror)]
    source = jnp.where(half_index == traded, 2 * mirror + half_index, block_ids).astype(jnp.int32)
    return context[source].reshape(total_rows, head_count * head_width)
```

```python
import jax
import jax.numpy as jnp
import numpy as np
from jax import lax
from jax.experimental import pallas as pl
from jax.experimental.pallas import tpu as pltpu
from jax.sharding import PartitionSpec as P

NX, NZ, NY = 2, 8, 4
TOK = 192
BLK = 96
HEADS, DH = 8, 128
ROWS = BLK * HEADS
RA, RB = 128, 64
TILE = 256
HT = 2
RT = BLK * HT
SCALE = float(np.log2(np.e) / np.sqrt(DH))
UNSEEN = -1e30
NO_MAX = -1e20


def dev(x, z, y):
    return (x % NX) * 32 + (z % NZ) * 4 + (y % NY)


def shift(dx, dz, dy):
    return [
        (dev(x, z, y), dev(x + dx, z + dz, y + dy))
        for x in range(NX)
        for z in range(NZ)
        for y in range(NY)
    ]


Z_LINES = [[dev(x, z, y) for z in range(NZ)] for x in range(NX) for y in range(NY)]
XY_PLANES = [[dev(x, z, y) for x in range(NX) for y in range(NY)] for z in range(NZ)]
MIRROR = [(d, 63 - d) for d in range(64)]

A_POS = np.concatenate([z * 768 + np.arange(RA) for z in range(NZ)])
B_POS = np.concatenate([x * 6144 + y * TOK + RA + np.arange(RB) for x in range(NX) for y in range(NY)])


def kernel(kinds, first, last, *refs):
    n = len(kinds)
    scal, q_refs = refs[0], refs[1:3]
    refs = refs[3:]
    pos_a, pos_b = refs[:2]
    units, refs = refs[2 : 2 + n], refs[2 + n :]
    if not first:
        m_in, acc_in = refs[:2]
        refs = refs[2:]
    if last:
        out, m_ref, acc_ref, s_ref, mx_ref = refs
    else:
        m_ref, acc_ref, s_ref, mx_ref = refs
    if first:
        m_ref[...] = jnp.full(m_ref.shape, NO_MAX, jnp.float32)
        acc_ref[...] = jnp.zeros(acc_ref.shape, jnp.float32)
    elif last:
        m_ref[...] = m_in[...]
        acc_ref[...] = acc_in[...]

    for b in range(2):
        start = scal[b]
        q_ref = q_refs[b]
        for u, kind in enumerate(kinds):
            kv = units[u]
            table, pos_ref = (A_POS, pos_a) if kind == "a" else (B_POS, pos_b)
            tiles = len(table) // TILE
            offset = scal[2 + u]
            seen = 0
            for t in range(tiles):
                low = int(table[t * TILE])
                seen = seen + jnp.where(low + offset <= start + (BLK - 1), 1, 0)

            @pl.when(seen > 0)
            def _():
                for r in range(HEADS // HT):
                    mx_ref[pl.ds(r * RT, RT), :] = m_ref[pl.ds(b * ROWS + r * RT, RT), :]

                def score(t, _):
                    k = kv[pl.ds(pl.multiple_of(t * TILE, TILE), TILE), :DH]
                    for r in range(HEADS // HT):
                        q = jnp.concatenate(
                            [q_ref[:, (r * HT + h) * DH : (r * HT + h + 1) * DH] for h in range(HT)], axis=0
                        )
                        s = lax.dot_general(q, k, (((1,), (1,)), ((), ())), preferred_element_type=jnp.float32)
                        s_ref[t, pl.ds(r * RT, RT), :] = s

                        @pl.when(t < seen - 1)
                        def _():
                            m = jnp.maximum(s[:, :128], s[:, 128:])
                            mx_ref[pl.ds(r * RT, RT), :] = jnp.maximum(mx_ref[pl.ds(r * RT, RT), :], m)

                    return 0

                lax.fori_loop(0, seen, score, 0)
                t = seen - 1
                kpos = pos_ref[pl.ds(t, 1), :] + offset
                qpos = start + lax.broadcasted_iota(jnp.int32, (BLK, TILE), 0)
                bias = jnp.where(kpos <= qpos, 0.0, UNSEEN)
                bias = jnp.concatenate([bias] * HT, axis=0)
                for r in range(HEADS // HT):
                    rows = pl.ds(r * RT, RT)
                    s = s_ref[t, rows, :] + bias
                    s_ref[t, rows, :] = s
                    m = jnp.maximum(mx_ref[rows, :], jnp.maximum(s[:, :128], s[:, 128:]))
                    m = jnp.broadcast_to(jnp.max(m, axis=1, keepdims=True), (RT, 128))
                    at = pl.ds(b * ROWS + r * RT, RT)
                    alpha = jnp.exp2((m_ref[at, :] - m) * SCALE)
                    m_ref[at, :] = m
                    mx_ref[rows, :] = m
                    acc_ref[at, :] = acc_ref[at, :] * jnp.concatenate([alpha, alpha], axis=1)

                def weigh(t, _):
                    v = kv[pl.ds(pl.multiple_of(t * TILE, TILE), TILE), DH:]
                    v = jnp.concatenate([v, jnp.ones((TILE, DH), jnp.bfloat16)], axis=1)
                    for r in range(HEADS // HT):
                        rows = pl.ds(r * RT, RT)
                        at = pl.ds(b * ROWS + r * RT, RT)
                        m = mx_ref[rows, :]
                        p = jnp.exp2((s_ref[t, rows, :] - jnp.concatenate([m, m], axis=1)) * SCALE)
                        acc_ref[at, :] += jnp.dot(p.astype(jnp.bfloat16), v, preferred_element_type=jnp.float32)
                    return 0

                lax.fori_loop(0, seen, weigh, 0)

        if last:
            row = pl.multiple_of(scal[2 + n + b], 32)
            for h in range(HEADS):
                at = pl.ds(b * ROWS + h * BLK, BLK)
                ctx = acc_ref[at, :DH] / acc_ref[at, DH:]
                out[pl.ds(row, BLK), h * DH : (h + 1) * DH] = ctx.astype(jnp.bfloat16)


def absorb(kinds, scal, queries, tables, units, state, last):
    first = state is None
    vmem = pl.BlockSpec(memory_space=pltpu.VMEM)
    ops = [scal, *queries, *tables, *units] + ([] if first else list(state))
    m_shape = (2 * ROWS, 128)
    acc_shape = (2 * ROWS, 2 * DH)
    scratch = [pltpu.VMEM((4, ROWS, TILE), jnp.float32), pltpu.VMEM((ROWS, 128), jnp.float32)]
    aliases = {}
    if last:
        out_shape = jax.ShapeDtypeStruct((TOK, HEADS * DH), jnp.bfloat16)
        out_specs = vmem
        scratch = [pltpu.VMEM(m_shape, jnp.float32), pltpu.VMEM(acc_shape, jnp.float32)] + scratch
    else:
        out_shape = (jax.ShapeDtypeStruct(m_shape, jnp.float32), jax.ShapeDtypeStruct(acc_shape, jnp.float32))
        out_specs = (vmem, vmem)
        if not first:
            aliases = {len(ops) - 2: 0, len(ops) - 1: 1}
    keys = sum(1024 if k == "a" else 512 for k in kinds)
    return pl.pallas_call(
        lambda *refs: kernel(kinds, first, last, *refs),
        out_shape=out_shape,
        in_specs=[pl.BlockSpec(memory_space=pltpu.SMEM)] + [vmem] * (len(ops) - 1),
        out_specs=out_specs,
        scratch_shapes=scratch,
        input_output_aliases=aliases,
        compiler_params=pltpu.CompilerParams(vmem_limit_bytes=32 * 1024 * 1024),
        cost_estimate=pl.CostEstimate(
            flops=2 * ROWS * keys * DH * 2, bytes_accessed=4 << 20, transcendentals=ROWS * keys
        ),
        name="absorb",
    )(*ops)


def local(queries, keys, values, steal_block):
    place = lax.axis_index("ctx")
    mirror = 63 - place
    px, pz, py = place // 32, (place // NY) % NZ, place % NY
    traded = steal_block[jnp.minimum(place, mirror)]
    kept = 1 - traded
    kv = jnp.concatenate([keys, values], axis=1)
    own = lax.dynamic_slice_in_dim(queries, traded * BLK, BLK, 0)
    own = lax.ppermute(own, "ctx", MIRROR)
    stay = lax.dynamic_slice_in_dim(queries, kept * BLK, BLK, 0)
    start0 = mirror * TOK + traded * BLK
    start1 = place * TOK + kept * BLK

    def send(array, dx, dz, dy):
        return lax.ppermute(array, "ctx", shift(dx, dz, dy))

    kv_b = lax.all_to_all(
        jnp.broadcast_to(kv[None, RA:], (NX * NY, RB, 2 * DH)).reshape(NX * NY * RB, 2 * DH),
        "ctx", 0, 0, axis_index_groups=XY_PLANES, tiled=True,
    )
    kv_a = lax.all_to_all(
        jnp.broadcast_to(kv[None, :RA], (NZ, RA, 2 * DH)).reshape(NZ * RA, 2 * DH),
        "ctx", 0, 0, axis_index_groups=Z_LINES, tiled=True,
    )

    def off_a(dx, dy):
        return ((px + dx) % NX * 32 + (py + dy) % NY) * TOK

    def off_b(dz):
        return (pz + dz) % NZ * NY * TOK

    tables = (jnp.asarray(A_POS.reshape(-1, TILE), jnp.int32), jnp.asarray(B_POS.reshape(-1, TILE), jnp.int32))
    both = (own, stay)

    def step(units, state, last=False):
        kinds = tuple(k for k, _, _ in units)
        scal = [start0, start1] + [o for _, _, o in units]
        if last:
            scal += [traded * BLK, kept * BLK]
        scal = jnp.stack([jnp.asarray(s, jnp.int32) for s in scal])
        return absorb(kinds, scal, both, tables, [a for _, a, _ in units], state, last)

    up = {0: kv_b}
    for d in (1, 2, 3):
        up[d] = send(up[d - 1], 0, -1, 0)
        up[-d] = send(up[-(d - 1)], 0, 1, 0)
    half = NX * NY * RB // 2
    far = jnp.concatenate([send(up[3][:half], 0, -1, 0), send(up[-3][half:], 0, 1, 0)], axis=0)

    xa = send(kv_a, 1, 0, 0)
    yp = send(kv_a, 0, 0, -1)
    ym = send(kv_a, 0, 0, 1)
    xyp = send(yp, 1, 0, 0)
    y2 = send(yp, 0, 0, -1)
    xym = send(xa, 0, 0, 1)
    third = [0, 336, 672, 1024]
    xy2 = jnp.concatenate(
        [
            send(y2[: third[1]], 1, 0, 0),
            send(xyp[third[1] : third[2]], 0, 0, -1),
            send(xym[third[2] :], 0, 0, 1),
        ],
        axis=0,
    )

    state = step([("b", up[0], off_b(0)), ("a", kv_a, off_a(0, 0))], None)
    state = step([("b", up[1], off_b(1)), ("b", up[-1], off_b(-1))], state)
    state = step([("a", xa, off_a(1, 0)), ("a", yp, off_a(0, 1)), ("a", ym, off_a(0, -1))], state)
    state = step([("b", up[2], off_b(2)), ("b", up[-2], off_b(-2)), ("b", up[3], off_b(3)), ("b", up[-3], off_b(-3))], state)
    state = step([("a", xyp, off_a(1, 1)), ("a", y2, off_a(0, 2)), ("a", xym, off_a(1, -1))], state)
    return step([("b", far, off_b(4)), ("a", xy2, off_a(1, 2))], state, last=True)


def solution(mesh):
    placed = (P(("batch", "ctx"), None), P(("batch", "ctx"), None), P(("batch", "ctx"), None), P())
    return jax.shard_map(
        local, mesh=mesh, in_specs=placed, out_specs=P(("batch", "ctx"), None), check_vma=False
    )
```

```python
import functools

import jax
import jax.numpy as jnp
import numpy as np
from jax import lax
from jax.experimental import pallas as pl
from jax.experimental.pallas import tpu as pltpu
from jax.sharding import PartitionSpec as P

NX, NZ, NY = 2, 8, 4
TOK = 192
BLK = 96
HEADS, DH = 8, 128
ROWS = BLK * HEADS
RA, RB = 128, 64
TILE = 256
GROUP = 8
MAX_TILES = 16
NOWHERE = 1 << 20
COST = 8
HT = 4
RT = BLK * HT
SCALE = float(np.log2(np.e) / np.sqrt(DH))
UNSEEN = -1e30
NO_MAX = -1e20


def dev(x, z, y):
    return (x % NX) * 32 + (z % NZ) * 4 + (y % NY)


def shift(dx, dz, dy):
    return [
        (dev(x, z, y), dev(x + dx, z + dz, y + dy))
        for x in range(NX)
        for z in range(NZ)
        for y in range(NY)
    ]


Z_LINES = [[dev(x, z, y) for z in range(NZ)] for x in range(NX) for y in range(NY)]
XY_PLANES = [[dev(x, z, y) for x in range(NX) for y in range(NY)] for z in range(NZ)]
MIRROR = [(d, 63 - d) for d in range(64)]

def tile_base(kind, t, base):
    return base + t * (2 * 768 if kind == "a" else 32 * TOK)


def whereabouts(steal_ref):
    place = lax.axis_index("ctx")
    return place, steal_ref[jnp.minimum(place, 63 - place)]


def kernel(kinds, bases, first, last, *refs):
    n = len(kinds)
    steal_ref = refs[0]
    units, refs = refs[1 : 1 + n], refs[1 + n :]
    if first:
        own_ref, kept_ref, q_ref = refs[0], refs[1], refs[2]
        refs = refs[3:]
    else:
        q_ref, m_in, l_in, acc_in = refs[:4]
        refs = refs[4:]
    if last:
        out = refs[0]
        refs = refs[1:]
    m_ref, l_ref, acc_ref, kv_ref, pos_ref, low_ref, kind_ref, list_ref, sem = refs
    copies, tiles = [], []
    for u, kind in enumerate(kinds):
        count = (NZ * RA if kind == "a" else NX * NY * RB) // TILE
        copies.append(pltpu.make_async_copy(units[u], kv_ref.at[pl.ds(len(tiles) * TILE, count * TILE)], sem.at[u]))
        copies[-1].start()
        tiles += [(u, kind, t) for t in range(count)]
    place, traded = whereabouts(steal_ref)
    if first:
        for h in range(HEADS):
            cols = pl.ds(h * DH, DH)
            q_ref[pl.ds(h * BLK, BLK), :] = own_ref[:, cols]
            q_ref[pl.ds(ROWS + h * BLK, BLK), :] = kept_ref[:, cols]
        m_ref[...] = jnp.full(m_ref.shape, NO_MAX, jnp.float32)
        l_ref[...] = jnp.zeros(l_ref.shape, jnp.float32)
        acc_ref[...] = jnp.zeros(acc_ref.shape, jnp.float32)
    elif last:
        m_ref[...] = m_in[...]
        l_ref[...] = l_in[...]
        acc_ref[...] = acc_in[...]
    key = lax.broadcasted_iota(jnp.int32, (1, TILE), 1)
    pos_ref[0:1, :] = key + key // RA * (NY * TOK - RA)
    pos_ref[1:2, :] = key + key // RB * (TOK - RB)
    x, z, y = place // 32, (place // NY) % NZ, place % NY
    starts = ((63 - place) * TOK + traded * BLK, place * TOK + (1 - traded) * BLK)
    total = len(tiles)
    counts = [0, 0]
    low_ref[total] = NOWHERE
    kind_ref[total] = 0
    for i, (u, kind, t) in enumerate(tiles):
        dx, dz, dy = bases[u]
        if kind == "a":
            base = ((x + dx) % NX * 32 + (y + dy + NY) % NY) * TOK
        else:
            base = (z + dz + NZ) % NZ * NY * TOK + RA
        low = tile_base(kind, t, base)
        low_ref[i] = low
        kind_ref[i] = 0 if kind == "a" else 1
        for b in range(2):
            list_ref[b * (MAX_TILES + 1) + counts[b]] = i
            counts[b] = counts[b] + jnp.where(low <= starts[b] + (BLK - 1), 1, 0)
    for b in range(2):
        list_ref[b * (MAX_TILES + 1) + counts[b]] = total
        counts[b] = counts[b] + jnp.where(counts[b] % 4 == 3, 1, 0)
    for c in copies:
        c.wait()

    def block(b, _):
        start = jnp.where(b == 0, starts[0], starts[1])
        count = jnp.where(b == 0, counts[0], counts[1])

        def group(at, size):
            index = [list_ref[b * (MAX_TILES + 1) + at + j] for j in range(size)]
            here = [pl.ds(pl.multiple_of(jnp.minimum(i, total - 1) * TILE, TILE), TILE) for i in index]
            k = jnp.concatenate([kv_ref[r, :DH] for r in here], axis=0)
            v = jnp.concatenate([kv_ref[r, DH:] for r in here], axis=0)
            kpos = jnp.concatenate([pos_ref[pl.ds(kind_ref[i], 1), :] + low_ref[i] for i in index], axis=1)
            qpos = start + lax.broadcasted_iota(jnp.int32, (BLK, size * TILE), 0)
            bias = jnp.where(kpos <= qpos, 0.0, UNSEEN)
            bias = jnp.concatenate([bias] * HT, axis=0)
            lanes = size * TILE // 128

            def rows(r):
                return pl.ds(pl.multiple_of(b * ROWS + r * RT, RT), RT)

            def score(r):
                q = q_ref[rows(r), :]
                return lax.dot_general(q, k, (((1,), (1,)), ((), ())), preferred_element_type=jnp.float32)

            def weigh(r, s):
                s = s + bias
                old = m_ref[rows(r), :]
                m = functools.reduce(jnp.maximum, [s[:, i * 128 : (i + 1) * 128] for i in range(lanes)])
                m = jnp.maximum(old, jnp.broadcast_to(jnp.max(m, axis=1, keepdims=True), (RT, 128)))
                m_ref[rows(r), :] = m
                alpha = jnp.exp2((old - m) * SCALE)
                p = jnp.exp2(s * SCALE - jnp.concatenate([m * SCALE] * lanes, axis=1))
                part = functools.reduce(jnp.add, [p[:, i * 128 : (i + 1) * 128] for i in range(lanes)])
                l_ref[rows(r), :] = l_ref[rows(r), :] * alpha + part
                return p.astype(jnp.bfloat16), alpha

            def add(r, p, alpha):
                acc_ref[rows(r), :] = acc_ref[rows(r), :] * alpha + jnp.dot(p, v, preferred_element_type=jnp.float32)

            steps = HEADS // HT
            s = score(0)
            done = None
            for r in range(steps):
                after = score(r + 1) if r + 1 < steps else None
                weighed = weigh(r, s)
                if done is not None:
                    add(r - 1, *done)
                done, s = weighed, after
            add(steps - 1, *done)

        def whole(g, _):
            group(g * GROUP, GROUP)
            return 0

        lax.fori_loop(0, count // GROUP, whole, 0)
        size = GROUP // 2
        while size:

            @pl.when(count // size % 2 == 1)
            def _(size=size):
                group(count // (2 * size) * (2 * size), size)

            size //= 2

        if last:
            row = pl.multiple_of(jnp.where(b == 0, traded, 1 - traded) * BLK, 32)
            for h in range(HEADS):
                at = pl.ds(pl.multiple_of(b * ROWS + h * BLK, BLK), BLK)
                ctx = acc_ref[at, :] / jnp.sum(l_ref[at, :], axis=1, keepdims=True)
                out[pl.ds(row, BLK), h * DH : (h + 1) * DH] = ctx.astype(jnp.bfloat16)
        return 0

    lax.fori_loop(0, 2, block, 0)


def absorb(units, steal_block, state, last=False):
    kinds = tuple(k for k, _, _ in units)
    bases = tuple(o for _, _, o in units)
    first = len(state) == 2
    vmem = pl.BlockSpec(memory_space=pltpu.VMEM)
    ops = [steal_block] + [a for _, a, _ in units] + list(state)
    shape = jax.ShapeDtypeStruct((2 * ROWS, DH), jnp.float32)
    keys = sum(NZ * RA if k == "a" else NX * NY * RB for k in kinds)
    count = keys // TILE
    scratch = [
        pltpu.VMEM((keys, 2 * DH), jnp.bfloat16),
        pltpu.VMEM((8, TILE), jnp.int32),
        pltpu.SMEM((count + 1,), jnp.int32),
        pltpu.SMEM((count + 1,), jnp.int32),
        pltpu.SMEM((2 * (MAX_TILES + 1),), jnp.int32),
        pltpu.SemaphoreType.DMA((len(kinds),)),
    ]
    aliases = {}
    if last:
        out_shape = jax.ShapeDtypeStruct((TOK, HEADS * DH), jnp.bfloat16)
        out_specs = vmem
        scratch = [pltpu.VMEM(shape.shape, jnp.float32)] * 3 + scratch
    else:
        out_shape, out_specs = (shape,) * 3, (vmem,) * 3
        if first:
            out_shape = (jax.ShapeDtypeStruct((2 * ROWS, DH), jnp.bfloat16),) + out_shape
            out_specs = (vmem,) * 4
        else:
            aliases = {len(ops) - 3 + i: i for i in range(3)}
    got = pl.pallas_call(
        functools.partial(kernel, kinds, bases, first, last),
        out_shape=out_shape,
        in_specs=[pl.BlockSpec(memory_space=pltpu.SMEM)]
        + [pl.BlockSpec(memory_space=pl.ANY)] * len(kinds)
        + [vmem] * len(state),
        out_specs=out_specs,
        scratch_shapes=scratch,
        input_output_aliases=aliases,
        compiler_params=pltpu.CompilerParams(vmem_limit_bytes=32 * 1024 * 1024),
        cost_estimate=pl.CostEstimate(
            flops=COST * 2 * ROWS * keys * DH * 2, bytes_accessed=4 << 20, transcendentals=ROWS * keys
        ),
        name="absorb",
    )(*ops)
    return got if first or last else (state[0], *got)


def pack_kernel(keys_ref, values_ref, a_ref, b_ref):
    for i in range(NZ):
        a_ref[pl.ds(i * RA, RA), :DH] = keys_ref[:RA, :]
        a_ref[pl.ds(i * RA, RA), DH:] = values_ref[:RA, :]
    for i in range(NX * NY):
        b_ref[pl.ds(i * RB, RB), :DH] = keys_ref[RA:, :]
        b_ref[pl.ds(i * RB, RB), DH:] = values_ref[RA:, :]


def pack(keys, values):
    vmem = pl.BlockSpec(memory_space=pltpu.VMEM)
    return pl.pallas_call(
        pack_kernel,
        out_shape=(
            jax.ShapeDtypeStruct((NZ * RA, 2 * DH), jnp.bfloat16),
            jax.ShapeDtypeStruct((NX * NY * RB, 2 * DH), jnp.bfloat16),
        ),
        in_specs=[vmem] * 2,
        out_specs=(vmem,) * 2,
        name="pack",
    )(keys, values)


def part_kernel(steal_ref, queries_ref, own_ref, kept_ref, sem):
    _, traded = whereabouts(steal_ref)
    copies = []
    for i, (ref, b) in enumerate(((own_ref, traded), (kept_ref, 1 - traded))):
        rows = pl.ds(pl.multiple_of(b * BLK, 32), BLK)
        copies.append(pltpu.make_async_copy(queries_ref.at[rows], ref, sem.at[i]))
        copies[-1].start()
    for c in copies:
        c.wait()


def part(steal_block, queries):
    vmem = pl.BlockSpec(memory_space=pltpu.VMEM)
    return pl.pallas_call(
        part_kernel,
        out_shape=(jax.ShapeDtypeStruct((BLK, HEADS * DH), jnp.bfloat16),) * 2,
        in_specs=[pl.BlockSpec(memory_space=pltpu.SMEM), pl.BlockSpec(memory_space=pl.ANY)],
        out_specs=(vmem,) * 2,
        scratch_shapes=[pltpu.SemaphoreType.DMA((2,))],
        name="part",
    )(steal_block, queries)


def together(*arrays):
    return pl.pallas_call(
        lambda *refs: None,
        out_shape=tuple(jax.ShapeDtypeStruct(a.shape, a.dtype) for a in arrays),
        in_specs=[pl.BlockSpec(memory_space=pl.ANY)] * len(arrays),
        out_specs=(pl.BlockSpec(memory_space=pl.ANY),) * len(arrays),
        input_output_aliases={i: i for i in range(len(arrays))},
        name="together",
    )(*arrays)


def local(queries, keys, values, steal_block):
    sent_a, sent_b = pack(keys, values)
    sent_q, kept = part(steal_block, queries)

    def send(array, dx, dz, dy):
        return lax.ppermute(array, "ctx", shift(dx, dz, dy))

    def step(units, state, last=False):
        return absorb(units, steal_block, state, last)

    kv_a = lax.all_to_all(sent_a, "ctx", 0, 0, axis_index_groups=Z_LINES, tiled=True)
    kv_a, sent_b, sent_q = together(kv_a, sent_b, sent_q)
    xa = send(kv_a, 1, 0, 0)
    yp = send(kv_a, 0, 0, -1)
    ym = send(kv_a, 0, 0, 1)
    xyp = send(yp, 1, 0, 0)
    y2 = send(yp, 0, 0, -1)
    xym = send(xa, 0, 0, 1)
    xy2 = send(y2, 1, 0, 0)
    own = lax.ppermute(sent_q, "ctx", MIRROR)

    ring = {0: lax.all_to_all(sent_b, "ctx", 0, 0, axis_index_groups=XY_PLANES, tiled=True)}
    for d in (1, 2):
        ring[d] = send(ring[0], 0, -d, 0)
        ring[-d] = send(ring[0], 0, d, 0)
    ring[3] = send(ring[2], 0, -1, 0)
    ring[-3] = send(ring[-2], 0, 1, 0)
    ring[4] = send(ring[2], 0, -2, 0)

    def far(*ds):
        return [("b", ring[d], (0, d, 0)) for d in ds]

    state = step([("a", kv_a, (0, 0, 0))], (own, kept))
    state = step([("a", xa, (1, 0, 0)), ("a", yp, (0, 0, 1)), ("a", ym, (0, 0, -1)), *far(0)], state)
    state = step([("a", xyp, (1, 0, 1)), ("a", y2, (0, 0, 2)), ("a", xym, (1, 0, -1)), *far(1, -1)], state)
    return step([("a", xy2, (1, 0, 2)), *far(2, -2, 3, -3, 4)], state, last=True)


def solution(mesh):
    placed = (P(("batch", "ctx"), None), P(("batch", "ctx"), None), P(("batch", "ctx"), None), P())
    return jax.shard_map(
        local, mesh=mesh, in_specs=placed, out_specs=P(("batch", "ctx"), None), check_vma=False
    )
```

```python
import functools

import jax
import jax.numpy as jnp
import numpy as np
from jax import lax
from jax.experimental import pallas as pl
from jax.experimental.pallas import tpu as pltpu
from jax.sharding import PartitionSpec as P

NX, NZ, NY = 2, 8, 4
TOK = 192
BLK = 96
HEADS, DH = 8, 128
ROWS = BLK * HEADS
RA, RB = 128, 64
TILE = 256
GROUP = 8
MAX_TILES = 24
SMALL = pltpu.CompilerParams(vmem_limit_bytes=6 * 1024 * 1024)
NOWHERE = 1 << 20
COST = 8
HT = 4
RT = BLK * HT
SCALE = float(np.log2(np.e) / np.sqrt(DH))
UNSEEN = -1e30
NO_MAX = -1e20


def dev(x, z, y):
    return (x % NX) * 32 + (z % NZ) * 4 + (y % NY)


def shift(dx, dz, dy):
    return [
        (dev(x, z, y), dev(x + dx, z + dz, y + dy))
        for x in range(NX)
        for z in range(NZ)
        for y in range(NY)
    ]


Z_LINES = [[dev(x, z, y) for z in range(NZ)] for x in range(NX) for y in range(NY)]
XY_PLANES = [[dev(x, z, y) for x in range(NX) for y in range(NY)] for z in range(NZ)]
PLANE = [(dx, dy) for dx in range(NX) for dy in range(NY)]
MIRROR = [(d, 63 - d) for d in range(64)]

def tile_base(kind, t, base):
    return base + t * (2 * 768 if kind == "a" else 32 * TOK)


def whereabouts(steal_ref):
    place = lax.axis_index("ctx")
    return place, steal_ref[jnp.minimum(place, 63 - place)]


def kernel(kinds, bases, first, last, *refs):
    n = len(kinds)
    steal_ref = refs[0]
    units, refs = refs[1 : 1 + n], refs[1 + n :]
    if first:
        own_ref, kept_ref, q_ref = refs[0], refs[1], refs[2]
        refs = refs[3:]
    else:
        q_ref, m_in, l_in, acc_in = refs[:4]
        refs = refs[4:]
    if last:
        out = refs[0]
        refs = refs[1:]
    m_ref, l_ref, acc_ref, kv_ref, pos_ref, low_ref, kind_ref, list_ref, sem = refs[:9]
    if first:
        raw_ref, raw_sem = refs[9:]
        fetch = [pltpu.make_async_copy(r, raw_ref.at[i], raw_sem.at[i]) for i, r in enumerate((own_ref, kept_ref))]
        for c in fetch:
            c.start()
    copies, tiles = [], []
    for u, kind in enumerate(kinds):
        count = (NZ * RA if kind == "a" else NX * NY * RB) // TILE
        copies.append(pltpu.make_async_copy(units[u], kv_ref.at[pl.ds(len(tiles) * TILE, count * TILE)], sem.at[u]))
        copies[-1].start()
        tiles += [(u, kind, t) for t in range(count)]
    place, traded = whereabouts(steal_ref)
    if first:
        m_ref[...] = jnp.full(m_ref.shape, NO_MAX, jnp.float32)
        l_ref[...] = jnp.zeros(l_ref.shape, jnp.float32)
        acc_ref[...] = jnp.zeros(acc_ref.shape, jnp.float32)
    elif last:
        m_ref[...] = m_in[...]
        l_ref[...] = l_in[...]
        acc_ref[...] = acc_in[...]
    key = lax.broadcasted_iota(jnp.int32, (1, TILE), 1)
    pos_ref[0:1, :] = key + key // RA * (NY * TOK - RA)
    pos_ref[1:2, :] = key + key // RB * (TOK - RB)
    x, z, y = place // 32, (place // NY) % NZ, place % NY
    starts = ((63 - place) * TOK + traded * BLK, place * TOK + (1 - traded) * BLK)
    total = len(tiles)
    counts = [0, 0]
    low_ref[total] = NOWHERE
    kind_ref[total] = 0
    for i, (u, kind, t) in enumerate(tiles):
        dx, dz, dy = bases[u]
        if kind == "a":
            base = ((x + dx) % NX * 32 + (y + dy + NY) % NY) * TOK
        else:
            base = (z + dz + NZ) % NZ * NY * TOK + RA
        low = tile_base(kind, t, base)
        low_ref[i] = low
        kind_ref[i] = 0 if kind == "a" else 1
        for b in range(2):
            list_ref[b * (MAX_TILES + 1) + counts[b]] = i
            counts[b] = counts[b] + jnp.where(low <= starts[b] + (BLK - 1), 1, 0)
    for b in range(2):
        list_ref[b * (MAX_TILES + 1) + counts[b]] = total
        counts[b] = counts[b] + jnp.where(counts[b] % 4 == 3, 1, 0)
    if first:
        for c in fetch:
            c.wait()
        for b in range(2):
            for h in range(HEADS):
                q_ref[pl.ds(b * ROWS + h * BLK, BLK), :] = raw_ref[b, :, pl.ds(h * DH, DH)]
    for c in copies:
        c.wait()

    def block(b, _):
        start = jnp.where(b == 0, starts[0], starts[1])
        count = jnp.where(b == 0, counts[0], counts[1])

        def group(at, size):
            index = [list_ref[b * (MAX_TILES + 1) + at + j] for j in range(size)]
            here = [pl.ds(pl.multiple_of(jnp.minimum(i, total - 1) * TILE, TILE), TILE) for i in index]
            k = jnp.concatenate([kv_ref[r, :DH] for r in here], axis=0)
            v = jnp.concatenate([kv_ref[r, DH:] for r in here], axis=0)
            kpos = jnp.concatenate([pos_ref[pl.ds(kind_ref[i], 1), :] + low_ref[i] for i in index], axis=1)
            qpos = start + lax.broadcasted_iota(jnp.int32, (BLK, size * TILE), 0)
            bias = jnp.where(kpos <= qpos, 0.0, UNSEEN)
            bias = jnp.concatenate([bias] * HT, axis=0)
            lanes = size * TILE // 128

            def rows(r):
                return pl.ds(pl.multiple_of(b * ROWS + r * RT, RT), RT)

            def score(r):
                q = q_ref[rows(r), :]
                return lax.dot_general(q, k, (((1,), (1,)), ((), ())), preferred_element_type=jnp.float32)

            def weigh(r, s):
                s = s + bias
                old = m_ref[rows(r), :]
                m = functools.reduce(jnp.maximum, [s[:, i * 128 : (i + 1) * 128] for i in range(lanes)])
                m = jnp.maximum(old, jnp.broadcast_to(jnp.max(m, axis=1, keepdims=True), (RT, 128)))
                m_ref[rows(r), :] = m
                alpha = jnp.exp2((old - m) * SCALE)
                p = jnp.exp2(s * SCALE - jnp.concatenate([m * SCALE] * lanes, axis=1))
                part = functools.reduce(jnp.add, [p[:, i * 128 : (i + 1) * 128] for i in range(lanes)])
                l_ref[rows(r), :] = l_ref[rows(r), :] * alpha + part
                return p.astype(jnp.bfloat16), alpha

            def add(r, p, alpha):
                acc_ref[rows(r), :] = acc_ref[rows(r), :] * alpha + jnp.dot(p, v, preferred_element_type=jnp.float32)

            steps = HEADS // HT
            s = score(0)
            done = None
            for r in range(steps):
                after = score(r + 1) if r + 1 < steps else None
                weighed = weigh(r, s)
                if done is not None:
                    add(r - 1, *done)
                done, s = weighed, after
            add(steps - 1, *done)

        def whole(g, _):
            group(g * GROUP, GROUP)
            return 0

        lax.fori_loop(0, count // GROUP, whole, 0)
        size = GROUP // 2
        while size:

            @pl.when(count // size % 2 == 1)
            def _(size=size):
                group(count // (2 * size) * (2 * size), size)

            size //= 2

        if last:
            row = pl.multiple_of(jnp.where(b == 0, traded, 1 - traded) * BLK, 32)
            for h in range(HEADS):
                at = pl.ds(pl.multiple_of(b * ROWS + h * BLK, BLK), BLK)
                ctx = acc_ref[at, :] / jnp.sum(l_ref[at, :], axis=1, keepdims=True)
                out[pl.ds(row, BLK), h * DH : (h + 1) * DH] = ctx.astype(jnp.bfloat16)
        return 0

    lax.fori_loop(0, 2, block, 0)


def absorb(units, steal_block, state, last=False):
    kinds = tuple(k for k, _, _ in units)
    bases = tuple(o for _, _, o in units)
    first = len(state) == 2
    vmem = pl.BlockSpec(memory_space=pltpu.VMEM)
    ops = [steal_block] + [a for _, a, _ in units] + list(state)
    shape = jax.ShapeDtypeStruct((2 * ROWS, DH), jnp.float32)
    keys = sum(NZ * RA if k == "a" else NX * NY * RB for k in kinds)
    count = keys // TILE
    scratch = [
        pltpu.VMEM((keys, 2 * DH), jnp.bfloat16),
        pltpu.VMEM((8, TILE), jnp.int32),
        pltpu.SMEM((count + 1,), jnp.int32),
        pltpu.SMEM((count + 1,), jnp.int32),
        pltpu.SMEM((2 * (MAX_TILES + 1),), jnp.int32),
        pltpu.SemaphoreType.DMA((len(kinds),)),
    ]
    if first:
        scratch += [pltpu.VMEM((2, BLK, HEADS * DH), jnp.bfloat16), pltpu.SemaphoreType.DMA((2,))]
    aliases = {}
    if last:
        out_shape = jax.ShapeDtypeStruct((TOK, HEADS * DH), jnp.bfloat16)
        out_specs = vmem
        scratch = [pltpu.VMEM(shape.shape, jnp.float32)] * 3 + scratch
    else:
        out_shape, out_specs = (shape,) * 3, (vmem,) * 3
        if first:
            out_shape = (jax.ShapeDtypeStruct((2 * ROWS, DH), jnp.bfloat16),) + out_shape
            out_specs = (vmem,) * 4
        else:
            aliases = {len(ops) - 3 + i: i for i in range(3)}
    got = pl.pallas_call(
        functools.partial(kernel, kinds, bases, first, last),
        out_shape=out_shape,
        in_specs=[pl.BlockSpec(memory_space=pltpu.SMEM)]
        + [pl.BlockSpec(memory_space=pl.ANY)] * len(kinds)
        + [pl.BlockSpec(memory_space=pl.ANY) if first else vmem] * len(state),
        out_specs=out_specs,
        scratch_shapes=scratch,
        input_output_aliases=aliases,
        compiler_params=pltpu.CompilerParams(vmem_limit_bytes=24 * 1024 * 1024),
        cost_estimate=pl.CostEstimate(
            flops=COST * 2 * ROWS * keys * DH * 2, bytes_accessed=4 << 20, transcendentals=ROWS * keys
        ),
        name="absorb",
    )(*ops)
    return got if first or last else (state[0], *got)


def pack_kernel(keys_ref, values_ref, a_ref, b_ref):
    for i in range(NZ):
        a_ref[pl.ds(i * RA, RA), :DH] = keys_ref[:RA, :]
        a_ref[pl.ds(i * RA, RA), DH:] = values_ref[:RA, :]
    b_ref[:, :DH] = keys_ref[RA:, :]
    b_ref[:, DH:] = values_ref[RA:, :]


def pack(keys, values):
    vmem = pl.BlockSpec(memory_space=pltpu.VMEM)
    return pl.pallas_call(
        pack_kernel,
        out_shape=(
            jax.ShapeDtypeStruct((NZ * RA, 2 * DH), jnp.bfloat16),
            jax.ShapeDtypeStruct((RB, 2 * DH), jnp.bfloat16),
        ),
        in_specs=[vmem] * 2,
        out_specs=(vmem,) * 2,
        compiler_params=SMALL,
        name="pack",
    )(keys, values)


def part_kernel(steal_ref, queries_ref, own_ref, kept_ref, sem):
    _, traded = whereabouts(steal_ref)
    copies = []
    for i, (ref, b) in enumerate(((own_ref, traded), (kept_ref, 1 - traded))):
        rows = pl.ds(pl.multiple_of(b * BLK, 32), BLK)
        copies.append(pltpu.make_async_copy(queries_ref.at[rows], ref, sem.at[i]))
        copies[-1].start()
    for c in copies:
        c.wait()


def part(steal_block, queries):
    vmem = pl.BlockSpec(memory_space=pltpu.VMEM)
    return pl.pallas_call(
        part_kernel,
        out_shape=(jax.ShapeDtypeStruct((BLK, HEADS * DH), jnp.bfloat16),) * 2,
        in_specs=[pl.BlockSpec(memory_space=pltpu.SMEM), pl.BlockSpec(memory_space=pl.ANY)],
        out_specs=(vmem,) * 2,
        scratch_shapes=[pltpu.SemaphoreType.DMA((2,))],
        compiler_params=SMALL,
        name="part",
    )(steal_block, queries)


def plane_kernel(*refs):
    n, more = NX * NY, (len(refs) - NX * NY - 2) // 2
    pieces, others, out, sem = refs[:n], refs[n : n + more], refs[n + more], refs[-1]
    place = lax.axis_index("ctx")
    x, y = place // 32, place % NY
    moves = list(zip(others, refs[n + more + 1 : -1]))
    for i, (dx, dy) in enumerate(PLANE):
        slot = (x + dx) % NX * NY + (y + dy) % NY
        moves.append((pieces[i], out.at[pl.ds(pl.multiple_of(slot * RB, RB), RB)]))
    copies = []
    for i, (source, target) in enumerate(moves):
        copies.append(pltpu.make_async_copy(source, target, sem.at[i]))
        copies[-1].start()
    for c in copies:
        c.wait()


def plane(pieces, *others):
    n = len(pieces)
    return pl.pallas_call(
        plane_kernel,
        out_shape=(jax.ShapeDtypeStruct((n * RB, 2 * DH), jnp.bfloat16),)
        + tuple(jax.ShapeDtypeStruct(a.shape, a.dtype) for a in others),
        in_specs=[pl.BlockSpec(memory_space=pl.ANY)] * (n + len(others)),
        out_specs=(pl.BlockSpec(memory_space=pltpu.VMEM),) * (1 + len(others)),
        scratch_shapes=[pltpu.SemaphoreType.DMA((n + len(others),))],
        compiler_params=SMALL,
        name="plane",
    )(*pieces, *others)


def local(queries, keys, values, steal_block):
    sent_a, sent_b = pack(keys, values)
    sent_q, kept = part(steal_block, queries)

    def send(array, dx, dz, dy):
        return lax.ppermute(array, "ctx", shift(dx, dz, dy))

    def step(units, state, last=False):
        return absorb(units, steal_block, state, last)

    kv_a = lax.all_to_all(sent_a, "ctx", 0, 0, axis_index_groups=Z_LINES, tiled=True)
    b = {(0, 0): sent_b}
    b[1, 0] = send(sent_b, 1, 0, 0)
    b[0, 1] = send(sent_b, 0, 0, -1)
    b[0, 3] = send(sent_b, 0, 0, 1)
    b[1, 1] = send(b[0, 1], 1, 0, 0)
    b[0, 2] = send(b[0, 1], 0, 0, -1)
    b[1, 3] = send(b[1, 0], 0, 0, 1)
    b[1, 2] = send(b[0, 2], 1, 0, 0)
    own = lax.ppermute(sent_q, "ctx", MIRROR)
    kv_b, kv_a, own, kept = plane([b[o] for o in PLANE], kv_a, own, kept)

    xa = send(kv_a, 1, 0, 0)
    yp = send(kv_a, 0, 0, -1)
    ym = send(kv_a, 0, 0, 1)
    xyp = send(yp, 1, 0, 0)
    y2 = send(yp, 0, 0, -1)
    xym = send(xa, 0, 0, 1)
    xy2 = send(y2, 1, 0, 0)

    ring = {0: kv_b}
    for d in (1, 2, 3):
        ring[d] = send(ring[d - 1], 0, -1, 0)
        ring[-d] = send(ring[1 - d], 0, 1, 0)
    ring[4] = send(ring[3], 0, -1, 0)

    def far(*ds):
        return [("b", ring[d], (0, d, 0)) for d in ds]

    state = step([("a", kv_a, (0, 0, 0)), *far(0)], (own, kept))
    near = [("a", xa, (1, 0, 0)), ("a", yp, (0, 0, 1)), ("a", ym, (0, 0, -1))]
    state = step([*near, *far(1, -1)], state)
    after = [("a", xyp, (1, 0, 1)), ("a", y2, (0, 0, 2)), ("a", xym, (1, 0, -1))]
    state = step([*after, *far(2, -2)], state)
    state = step(far(3, -3, 4), state)
    return step([("a", xy2, (1, 0, 2))], state, last=True)


def solution(mesh):
    placed = (P(("batch", "ctx"), None), P(("batch", "ctx"), None), P(("batch", "ctx"), None), P())
    return jax.shard_map(
        local, mesh=mesh, in_specs=placed, out_specs=P(("batch", "ctx"), None), check_vma=False
    )
```

```python
import functools

import jax
import jax.numpy as jnp
import numpy as np
from jax import lax
from jax.experimental import pallas as pl
from jax.experimental.pallas import tpu as pltpu
from jax.sharding import PartitionSpec as P

NX, NZ, NY = 2, 8, 4
TOK = 192
BLK = 96
HEADS, DH = 8, 128
ROWS = BLK * HEADS
RA, RB = 128, 64
TILE = 256
GROUP = 8
MAX_TILES = 24
SMALL = pltpu.CompilerParams(vmem_limit_bytes=6 * 1024 * 1024)
NOWHERE = 1 << 20
COST = 8
HT = 4
RT = BLK * HT
SCALE = float(np.log2(np.e) / np.sqrt(DH))
UNSEEN = -1e30
NO_MAX = -1e20


def dev(x, z, y):
    return (x % NX) * 32 + (z % NZ) * 4 + (y % NY)


def shift(dx, dz, dy):
    return [
        (dev(x, z, y), dev(x + dx, z + dz, y + dy))
        for x in range(NX)
        for z in range(NZ)
        for y in range(NY)
    ]


Z_LINES = [[dev(x, z, y) for z in range(NZ)] for x in range(NX) for y in range(NY)]
XY_PLANES = [[dev(x, z, y) for x in range(NX) for y in range(NY)] for z in range(NZ)]
PLANE = [(dx, dy) for dx in range(NX) for dy in range(NY)]
MIRROR = [(d, 63 - d) for d in range(64)]

def tile_base(kind, t, base):
    return base + t * (2 * 768 if kind == "a" else 32 * TOK)


def whereabouts(steal_ref):
    place = lax.axis_index("ctx")
    return place, steal_ref[jnp.minimum(place, 63 - place)]


def kernel(kinds, bases, first, last, *refs):
    n = len(kinds)
    steal_ref = refs[0]
    units, refs = refs[1 : 1 + n], refs[1 + n :]
    if first:
        own_ref, kept_ref, q_ref = refs[0], refs[1], refs[2]
        refs = refs[3:]
    else:
        q_ref, m_in, l_in, acc_in = refs[:4]
        refs = refs[4:]
    if last:
        out = refs[0]
        refs = refs[1:]
    m_ref, l_ref, acc_ref, kv_ref, pos_ref, low_ref, kind_ref, list_ref = refs[:8]
    tiles = []
    for u, kind in enumerate(kinds):
        count = (NZ * RA if kind == "a" else NX * NY * RB) // TILE
        kv_ref[pl.ds(len(tiles) * TILE, count * TILE), :] = units[u][...]
        tiles += [(u, kind, t) for t in range(count)]
    place, traded = whereabouts(steal_ref)
    if first:
        m_ref[...] = jnp.full(m_ref.shape, NO_MAX, jnp.float32)
        l_ref[...] = jnp.zeros(l_ref.shape, jnp.float32)
        acc_ref[...] = jnp.zeros(acc_ref.shape, jnp.float32)
    elif last:
        m_ref[...] = m_in[...]
        l_ref[...] = l_in[...]
        acc_ref[...] = acc_in[...]
    key = lax.broadcasted_iota(jnp.int32, (1, TILE), 1)
    pos_ref[0:1, :] = key + key // RA * (NY * TOK - RA)
    pos_ref[1:2, :] = key + key // RB * (TOK - RB)
    x, z, y = place // 32, (place // NY) % NZ, place % NY
    starts = ((63 - place) * TOK + traded * BLK, place * TOK + (1 - traded) * BLK)
    total = len(tiles)
    counts = [0, 0]
    low_ref[total] = NOWHERE
    kind_ref[total] = 0
    for i, (u, kind, t) in enumerate(tiles):
        dx, dz, dy = bases[u]
        if kind == "a":
            base = ((x + dx) % NX * 32 + (y + dy + NY) % NY) * TOK
        else:
            base = (z + dz + NZ) % NZ * NY * TOK + RA
        low = tile_base(kind, t, base)
        low_ref[i] = low
        kind_ref[i] = 0 if kind == "a" else 1
        for b in range(2):
            list_ref[b * (MAX_TILES + 1) + counts[b]] = i
            counts[b] = counts[b] + jnp.where(low <= starts[b] + (BLK - 1), 1, 0)
    for b in range(2):
        list_ref[b * (MAX_TILES + 1) + counts[b]] = total
        counts[b] = counts[b] + jnp.where(counts[b] % 4 == 3, 1, 0)
    if first:
        for b, ref in enumerate((own_ref, kept_ref)):
            for h in range(HEADS):
                q_ref[pl.ds(b * ROWS + h * BLK, BLK), :] = ref[:, h * DH : (h + 1) * DH]

    def block(b, _):
        start = jnp.where(b == 0, starts[0], starts[1])
        count = jnp.where(b == 0, counts[0], counts[1])

        def group(at, size):
            index = [list_ref[b * (MAX_TILES + 1) + at + j] for j in range(size)]
            here = [pl.ds(pl.multiple_of(jnp.minimum(i, total - 1) * TILE, TILE), TILE) for i in index]
            k = jnp.concatenate([kv_ref[r, :DH] for r in here], axis=0)
            v = jnp.concatenate([kv_ref[r, DH:] for r in here], axis=0)
            kpos = jnp.concatenate([pos_ref[pl.ds(kind_ref[i], 1), :] + low_ref[i] for i in index], axis=1)
            qpos = start + lax.broadcasted_iota(jnp.int32, (BLK, size * TILE), 0)
            bias = jnp.where(kpos <= qpos, 0.0, UNSEEN)
            bias = jnp.concatenate([bias] * HT, axis=0)
            lanes = size * TILE // 128

            def rows(r):
                return pl.ds(pl.multiple_of(b * ROWS + r * RT, RT), RT)

            def score(r):
                q = q_ref[rows(r), :]
                return lax.dot_general(q, k, (((1,), (1,)), ((), ())), preferred_element_type=jnp.float32)

            def weigh(r, s):
                s = s + bias
                old = m_ref[rows(r), :]
                m = functools.reduce(jnp.maximum, [s[:, i * 128 : (i + 1) * 128] for i in range(lanes)])
                m = jnp.maximum(old, jnp.broadcast_to(jnp.max(m, axis=1, keepdims=True), (RT, 128)))
                m_ref[rows(r), :] = m
                alpha = jnp.exp2((old - m) * SCALE)
                p = jnp.exp2(s * SCALE - jnp.concatenate([m * SCALE] * lanes, axis=1))
                part = functools.reduce(jnp.add, [p[:, i * 128 : (i + 1) * 128] for i in range(lanes)])
                l_ref[rows(r), :] = l_ref[rows(r), :] * alpha + part
                return p.astype(jnp.bfloat16), alpha

            def add(r, p, alpha):
                acc_ref[rows(r), :] = acc_ref[rows(r), :] * alpha + jnp.dot(p, v, preferred_element_type=jnp.float32)

            steps = HEADS // HT
            s = score(0)
            done = None
            for r in range(steps):
                after = score(r + 1) if r + 1 < steps else None
                weighed = weigh(r, s)
                if done is not None:
                    add(r - 1, *done)
                done, s = weighed, after
            add(steps - 1, *done)

        def whole(g, _):
            group(g * GROUP, GROUP)
            return 0

        lax.fori_loop(0, count // GROUP, whole, 0)
        size = GROUP // 2
        while size:

            @pl.when(count // size % 2 == 1)
            def _(size=size):
                group(count // (2 * size) * (2 * size), size)

            size //= 2

        if last:
            row = pl.multiple_of(jnp.where(b == 0, traded, 1 - traded) * BLK, 32)
            for h in range(HEADS):
                at = pl.ds(pl.multiple_of(b * ROWS + h * BLK, BLK), BLK)
                ctx = acc_ref[at, :] / jnp.sum(l_ref[at, :], axis=1, keepdims=True)
                out[pl.ds(row, BLK), h * DH : (h + 1) * DH] = ctx.astype(jnp.bfloat16)
        return 0

    lax.fori_loop(0, 2, block, 0)


def absorb(units, steal_block, state, last=False):
    kinds = tuple(k for k, _, _ in units)
    bases = tuple(o for _, _, o in units)
    first = len(state) == 2
    vmem = pl.BlockSpec(memory_space=pltpu.VMEM)
    ops = [steal_block] + [a for _, a, _ in units] + list(state)
    shape = jax.ShapeDtypeStruct((2 * ROWS, DH), jnp.float32)
    keys = sum(NZ * RA if k == "a" else NX * NY * RB for k in kinds)
    count = keys // TILE
    scratch = [
        pltpu.VMEM((keys, 2 * DH), jnp.bfloat16),
        pltpu.VMEM((8, TILE), jnp.int32),
        pltpu.SMEM((count + 1,), jnp.int32),
        pltpu.SMEM((count + 1,), jnp.int32),
        pltpu.SMEM((2 * (MAX_TILES + 1),), jnp.int32),
    ]
    aliases = {}
    if last:
        out_shape = jax.ShapeDtypeStruct((TOK, HEADS * DH), jnp.bfloat16)
        out_specs = vmem
        scratch = [pltpu.VMEM(shape.shape, jnp.float32)] * 3 + scratch
    else:
        out_shape, out_specs = (shape,) * 3, (vmem,) * 3
        if first:
            out_shape = (jax.ShapeDtypeStruct((2 * ROWS, DH), jnp.bfloat16),) + out_shape
            out_specs = (vmem,) * 4
        else:
            aliases = {len(ops) - 3 + i: i for i in range(3)}
    got = pl.pallas_call(
        functools.partial(kernel, kinds, bases, first, last),
        out_shape=out_shape,
        in_specs=[pl.BlockSpec(memory_space=pltpu.SMEM)]
        + [vmem] * (len(kinds) + len(state)),
        out_specs=out_specs,
        scratch_shapes=scratch,
        input_output_aliases=aliases,
        compiler_params=pltpu.CompilerParams(vmem_limit_bytes=24 * 1024 * 1024),
        cost_estimate=pl.CostEstimate(
            flops=COST * 2 * ROWS * keys * DH * 2, bytes_accessed=4 << 20, transcendentals=ROWS * keys
        ),
        name="absorb",
    )(*ops)
    return got if first or last else (state[0], *got)


def pack_kernel(keys_ref, values_ref, a_ref, b_ref):
    for i in range(NZ):
        a_ref[pl.ds(i * RA, RA), :DH] = keys_ref[:RA, :]
        a_ref[pl.ds(i * RA, RA), DH:] = values_ref[:RA, :]
    b_ref[:, :DH] = keys_ref[RA:, :]
    b_ref[:, DH:] = values_ref[RA:, :]


def pack(keys, values):
    vmem = pl.BlockSpec(memory_space=pltpu.VMEM)
    return pl.pallas_call(
        pack_kernel,
        out_shape=(
            jax.ShapeDtypeStruct((NZ * RA, 2 * DH), jnp.bfloat16),
            jax.ShapeDtypeStruct((RB, 2 * DH), jnp.bfloat16),
        ),
        in_specs=[vmem] * 2,
        out_specs=(vmem,) * 2,
        name="pack",
    )(keys, values)


def part_kernel(steal_ref, queries_ref, own_ref, kept_ref, sem):
    _, traded = whereabouts(steal_ref)
    copies = []
    for i, (ref, b) in enumerate(((own_ref, traded), (kept_ref, 1 - traded))):
        rows = pl.ds(pl.multiple_of(b * BLK, 32), BLK)
        copies.append(pltpu.make_async_copy(queries_ref.at[rows], ref, sem.at[i]))
        copies[-1].start()
    for c in copies:
        c.wait()


def part(steal_block, queries):
    vmem = pl.BlockSpec(memory_space=pltpu.VMEM)
    return pl.pallas_call(
        part_kernel,
        out_shape=(jax.ShapeDtypeStruct((BLK, HEADS * DH), jnp.bfloat16),) * 2,
        in_specs=[pl.BlockSpec(memory_space=pltpu.SMEM), pl.BlockSpec(memory_space=pl.ANY)],
        out_specs=(vmem,) * 2,
        scratch_shapes=[pltpu.SemaphoreType.DMA((2,))],
        compiler_params=SMALL,
        name="part",
    )(steal_block, queries)


def plane_kernel(*refs):
    n, more = NX * NY, (len(refs) - NX * NY - 2) // 2
    pieces, others, out, sem = refs[:n], refs[n : n + more], refs[n + more], refs[-1]
    place = lax.axis_index("ctx")
    x, y = place // 32, place % NY
    moves = list(zip(others, refs[n + more + 1 : -1]))
    for i, (dx, dy) in enumerate(PLANE):
        slot = (x + dx) % NX * NY + (y + dy) % NY
        moves.append((pieces[i], out.at[pl.ds(pl.multiple_of(slot * RB, RB), RB)]))
    copies = []
    for i, (source, target) in enumerate(moves):
        copies.append(pltpu.make_async_copy(source, target, sem.at[i]))
        copies[-1].start()
    for c in copies:
        c.wait()


def plane(pieces, *others):
    n = len(pieces)
    return pl.pallas_call(
        plane_kernel,
        out_shape=(jax.ShapeDtypeStruct((n * RB, 2 * DH), jnp.bfloat16),)
        + tuple(jax.ShapeDtypeStruct(a.shape, a.dtype) for a in others),
        in_specs=[pl.BlockSpec(memory_space=pl.ANY)] * (n + len(others)),
        out_specs=(pl.BlockSpec(memory_space=pltpu.VMEM),) * (1 + len(others)),
        scratch_shapes=[pltpu.SemaphoreType.DMA((n + len(others),))],
        compiler_params=SMALL,
        name="plane",
    )(*pieces, *others)


def local(queries, keys, values, steal_block):
    sent_a, sent_b = pack(keys, values)
    sent_q, kept = part(steal_block, queries)

    def send(array, dx, dz, dy):
        return lax.ppermute(array, "ctx", shift(dx, dz, dy))

    def step(units, state, last=False):
        return absorb(units, steal_block, state, last)

    kv_a = lax.all_to_all(sent_a, "ctx", 0, 0, axis_index_groups=Z_LINES, tiled=True)
    b = {(0, 0): sent_b}
    b[1, 0] = send(sent_b, 1, 0, 0)
    b[0, 1] = send(sent_b, 0, 0, -1)
    b[0, 3] = send(sent_b, 0, 0, 1)
    b[1, 1] = send(b[0, 1], 1, 0, 0)
    b[0, 2] = send(b[0, 1], 0, 0, -1)
    b[1, 3] = send(b[1, 0], 0, 0, 1)
    b[1, 2] = send(b[0, 2], 1, 0, 0)
    own = lax.ppermute(sent_q, "ctx", MIRROR)
    kv_b, kv_a, own, kept = plane([b[o] for o in PLANE], kv_a, own, kept)

    xa = send(kv_a, 1, 0, 0)
    yp = send(kv_a, 0, 0, -1)
    ym = send(kv_a, 0, 0, 1)
    xyp = send(yp, 1, 0, 0)
    y2 = send(yp, 0, 0, -1)
    xym = send(xa, 0, 0, 1)
    xy2 = send(y2, 1, 0, 0)

    ring = {0: kv_b}
    for d in (1, 2, 3):
        ring[d] = send(ring[d - 1], 0, -1, 0)
        ring[-d] = send(ring[1 - d], 0, 1, 0)
    ring[4] = send(ring[3], 0, -1, 0)

    def far(*ds):
        return [("b", ring[d], (0, d, 0)) for d in ds]

    state = step([("a", kv_a, (0, 0, 0)), *far(0)], (own, kept))
    near = [("a", xa, (1, 0, 0)), ("a", yp, (0, 0, 1)), ("a", ym, (0, 0, -1))]
    state = step([*near, *far(1, -1)], state)
    after = [("a", xyp, (1, 0, 1)), ("a", y2, (0, 0, 2)), ("a", xym, (1, 0, -1))]
    state = step([*after, *far(2, -2)], state)
    state = step(far(3, -3, 4), state)
    return step([("a", xy2, (1, 0, 2))], state, last=True)


def solution(mesh):
    placed = (P(("batch", "ctx"), None), P(("batch", "ctx"), None), P(("batch", "ctx"), None), P())
    return jax.shard_map(
        local, mesh=mesh, in_specs=placed, out_specs=P(("batch", "ctx"), None), check_vma=False
    )
```

```python
import functools

import jax
import jax.numpy as jnp
import numpy as np
from jax import lax
from jax.experimental import pallas as pl
from jax.experimental.pallas import tpu as pltpu
from jax.sharding import PartitionSpec as P

NX, NZ, NY = 2, 8, 4
TOK = 192
BLK = 96
HEADS, DH = 8, 128
ROWS = BLK * HEADS
RA, RB = 128, 64
TILE = 256
GROUP = 8
MAX_TILES = 24
SMALL = pltpu.CompilerParams(vmem_limit_bytes=6 * 1024 * 1024)
NOWHERE = 1 << 20
COST = 8
HT = 4
RT = BLK * HT
SCALE = float(np.log2(np.e) / np.sqrt(DH))
UNSEEN = -1e30
NO_MAX = -1e20


def dev(x, z, y):
    return (x % NX) * 32 + (z % NZ) * 4 + (y % NY)


def shift(dx, dz, dy):
    return [
        (dev(x, z, y), dev(x + dx, z + dz, y + dy))
        for x in range(NX)
        for z in range(NZ)
        for y in range(NY)
    ]


Z_LINES = [[dev(x, z, y) for z in range(NZ)] for x in range(NX) for y in range(NY)]
XY_PLANES = [[dev(x, z, y) for x in range(NX) for y in range(NY)] for z in range(NZ)]
PLANE = [(dx, dy) for dx in range(NX) for dy in range(NY)]
MIRROR = [(d, 63 - d) for d in range(64)]

def tile_base(kind, t, base):
    return base + t * (2 * 768 if kind == "a" else 32 * TOK)


def whereabouts(steal_ref):
    place = lax.axis_index("ctx")
    return place, steal_ref[jnp.minimum(place, 63 - place)]


def kernel(kinds, bases, first, last, *refs):
    n = len(kinds)
    steal_ref = refs[0]
    units, refs = refs[1 : 1 + n], refs[1 + n :]
    if first:
        own_ref, kept_ref, q_ref = refs[0], refs[1], refs[2]
        refs = refs[3:]
    else:
        q_ref, m_in, l_in, acc_in = refs[:4]
        refs = refs[4:]
    if last:
        out = refs[0]
        refs = refs[1:]
    m_ref, l_ref, acc_ref, kv_ref, pos_ref, low_ref, kind_ref, list_ref = refs[:8]
    tiles = []
    for u, kind in enumerate(kinds):
        count = (NZ * RA if kind == "a" else NX * NY * RB) // TILE
        kv_ref[pl.ds(len(tiles) * TILE, count * TILE), :] = units[u][...]
        tiles += [(u, kind, t) for t in range(count)]
    place, traded = whereabouts(steal_ref)
    if first:
        m_ref[...] = jnp.full(m_ref.shape, NO_MAX, jnp.float32)
        l_ref[...] = jnp.zeros(l_ref.shape, jnp.float32)
        acc_ref[...] = jnp.zeros(acc_ref.shape, jnp.float32)
    elif last:
        m_ref[...] = m_in[...]
        l_ref[...] = l_in[...]
        acc_ref[...] = acc_in[...]
    key = lax.broadcasted_iota(jnp.int32, (1, TILE), 1)
    pos_ref[0:1, :] = key + key // RA * (NY * TOK - RA)
    pos_ref[1:2, :] = key + key // RB * (TOK - RB)
    x, z, y = place // 32, (place // NY) % NZ, place % NY
    starts = ((63 - place) * TOK + traded * BLK, place * TOK + (1 - traded) * BLK)
    total = len(tiles)
    counts = [0, 0]
    low_ref[total] = NOWHERE
    kind_ref[total] = 0
    for i, (u, kind, t) in enumerate(tiles):
        dx, dz, dy = bases[u]
        if kind == "a":
            base = ((x + dx) % NX * 32 + (y + dy + NY) % NY) * TOK
        else:
            base = (z + dz + NZ) % NZ * NY * TOK + RA
        low = tile_base(kind, t, base)
        low_ref[i] = low
        kind_ref[i] = 0 if kind == "a" else 1
        for b in range(2):
            list_ref[b * (MAX_TILES + 1) + counts[b]] = i
            counts[b] = counts[b] + jnp.where(low <= starts[b] + (BLK - 1), 1, 0)
    for b in range(2):
        list_ref[b * (MAX_TILES + 1) + counts[b]] = total
        counts[b] = counts[b] + jnp.where(counts[b] % 4 == 3, 1, 0)
    if first:
        for b, ref in enumerate((own_ref, kept_ref)):
            for h in range(HEADS):
                q_ref[pl.ds(b * ROWS + h * BLK, BLK), :] = ref[:, h * DH : (h + 1) * DH]

    def block(b, _):
        start = jnp.where(b == 0, starts[0], starts[1])
        count = jnp.where(b == 0, counts[0], counts[1])

        def group(at, size):
            index = [list_ref[b * (MAX_TILES + 1) + at + j] for j in range(size)]
            here = [pl.ds(pl.multiple_of(jnp.minimum(i, total - 1) * TILE, TILE), TILE) for i in index]
            k = jnp.concatenate([kv_ref[r, :DH] for r in here], axis=0)
            v = jnp.concatenate([kv_ref[r, DH:] for r in here], axis=0)
            kpos = jnp.concatenate([pos_ref[pl.ds(kind_ref[i], 1), :] + low_ref[i] for i in index], axis=1)
            qpos = start + lax.broadcasted_iota(jnp.int32, (BLK, size * TILE), 0)
            bias = jnp.where(kpos <= qpos, 0.0, UNSEEN)
            bias = jnp.concatenate([bias] * HT, axis=0)
            lanes = size * TILE // 128

            def rows(r):
                return pl.ds(pl.multiple_of(b * ROWS + r * RT, RT), RT)

            def score(r):
                q = q_ref[rows(r), :]
                return lax.dot_general(q, k, (((1,), (1,)), ((), ())), preferred_element_type=jnp.float32)

            def weigh(r, s):
                s = s + bias
                old = m_ref[rows(r), :]
                m = functools.reduce(jnp.maximum, [s[:, i * 128 : (i + 1) * 128] for i in range(lanes)])
                m = jnp.maximum(old, jnp.broadcast_to(jnp.max(m, axis=1, keepdims=True), (RT, 128)))
                m_ref[rows(r), :] = m
                alpha = jnp.exp2((old - m) * SCALE)
                p = jnp.exp2(s * SCALE - jnp.concatenate([m * SCALE] * lanes, axis=1))
                part = functools.reduce(jnp.add, [p[:, i * 128 : (i + 1) * 128] for i in range(lanes)])
                l_ref[rows(r), :] = l_ref[rows(r), :] * alpha + part
                return p.astype(jnp.bfloat16), alpha

            def add(r, p, alpha):
                acc_ref[rows(r), :] = acc_ref[rows(r), :] * alpha + jnp.dot(p, v, preferred_element_type=jnp.float32)

            steps = HEADS // HT
            s = score(0)
            done = None
            for r in range(steps):
                after = score(r + 1) if r + 1 < steps else None
                weighed = weigh(r, s)
                if done is not None:
                    add(r - 1, *done)
                done, s = weighed, after
            add(steps - 1, *done)

        def whole(g, _):
            group(g * GROUP, GROUP)
            return 0

        lax.fori_loop(0, count // GROUP, whole, 0)
        size = GROUP // 2
        while size:

            @pl.when(count // size % 2 == 1)
            def _(size=size):
                group(count // (2 * size) * (2 * size), size)

            size //= 2

        if last:
            row = pl.multiple_of(jnp.where(b == 0, traded, 1 - traded) * BLK, 32)
            for h in range(HEADS):
                at = pl.ds(pl.multiple_of(b * ROWS + h * BLK, BLK), BLK)
                ctx = acc_ref[at, :] / jnp.sum(l_ref[at, :], axis=1, keepdims=True)
                out[pl.ds(row, BLK), h * DH : (h + 1) * DH] = ctx.astype(jnp.bfloat16)
        return 0

    lax.fori_loop(0, 2, block, 0)


def absorb(units, steal_block, state, last=False):
    kinds = tuple(k for k, _, _ in units)
    bases = tuple(o for _, _, o in units)
    first = len(state) == 2
    vmem = pl.BlockSpec(memory_space=pltpu.VMEM)
    ops = [steal_block] + [a for _, a, _ in units] + list(state)
    shape = jax.ShapeDtypeStruct((2 * ROWS, DH), jnp.float32)
    keys = sum(NZ * RA if k == "a" else NX * NY * RB for k in kinds)
    count = keys // TILE
    scratch = [
        pltpu.VMEM((keys, 2 * DH), jnp.bfloat16),
        pltpu.VMEM((8, TILE), jnp.int32),
        pltpu.SMEM((count + 1,), jnp.int32),
        pltpu.SMEM((count + 1,), jnp.int32),
        pltpu.SMEM((2 * (MAX_TILES + 1),), jnp.int32),
    ]
    aliases = {}
    if last:
        out_shape = jax.ShapeDtypeStruct((TOK, HEADS * DH), jnp.bfloat16)
        out_specs = vmem
        scratch = [pltpu.VMEM(shape.shape, jnp.float32)] * 3 + scratch
    else:
        out_shape, out_specs = (shape,) * 3, (vmem,) * 3
        if first:
            out_shape = (jax.ShapeDtypeStruct((2 * ROWS, DH), jnp.bfloat16),) + out_shape
            out_specs = (vmem,) * 4
        else:
            aliases = {len(ops) - 3 + i: i for i in range(3)}
    got = pl.pallas_call(
        functools.partial(kernel, kinds, bases, first, last),
        out_shape=out_shape,
        in_specs=[pl.BlockSpec(memory_space=pltpu.SMEM)]
        + [vmem] * (len(kinds) + len(state)),
        out_specs=out_specs,
        scratch_shapes=scratch,
        input_output_aliases=aliases,
        compiler_params=pltpu.CompilerParams(vmem_limit_bytes=24 * 1024 * 1024),
        cost_estimate=pl.CostEstimate(
            flops=COST * 2 * ROWS * keys * DH * 2, bytes_accessed=4 << 20, transcendentals=ROWS * keys
        ),
        name="absorb",
    )(*ops)
    return got if first or last else (state[0], *got)


def pack_kernel(keys_ref, values_ref, a_ref, b_ref):
    for i in range(NZ):
        a_ref[pl.ds(i * RA, RA), :DH] = keys_ref[:RA, :]
        a_ref[pl.ds(i * RA, RA), DH:] = values_ref[:RA, :]
    b_ref[:, :DH] = keys_ref[RA:, :]
    b_ref[:, DH:] = values_ref[RA:, :]


def pack(keys, values):
    vmem = pl.BlockSpec(memory_space=pltpu.VMEM)
    return pl.pallas_call(
        pack_kernel,
        out_shape=(
            jax.ShapeDtypeStruct((NZ * RA, 2 * DH), jnp.bfloat16),
            jax.ShapeDtypeStruct((RB, 2 * DH), jnp.bfloat16),
        ),
        in_specs=[vmem] * 2,
        out_specs=(vmem,) * 2,
        name="pack",
    )(keys, values)


def part_kernel(steal_ref, queries_ref, own_ref, kept_ref, sem):
    _, traded = whereabouts(steal_ref)
    copies = []
    for i, (ref, b) in enumerate(((own_ref, traded), (kept_ref, 1 - traded))):
        rows = pl.ds(pl.multiple_of(b * BLK, 32), BLK)
        copies.append(pltpu.make_async_copy(queries_ref.at[rows], ref, sem.at[i]))
        copies[-1].start()
    for c in copies:
        c.wait()


def part(steal_block, queries):
    vmem = pl.BlockSpec(memory_space=pltpu.VMEM)
    return pl.pallas_call(
        part_kernel,
        out_shape=(jax.ShapeDtypeStruct((BLK, HEADS * DH), jnp.bfloat16),) * 2,
        in_specs=[pl.BlockSpec(memory_space=pltpu.SMEM), pl.BlockSpec(memory_space=pl.ANY)],
        out_specs=(vmem,) * 2,
        scratch_shapes=[pltpu.SemaphoreType.DMA((2,))],
        compiler_params=SMALL,
        name="part",
    )(steal_block, queries)


def plane_kernel(*refs):
    n, more = NX * NY, (len(refs) - NX * NY - 2) // 2
    pieces, others, out, sem = refs[:n], refs[n : n + more], refs[n + more], refs[-1]
    place = lax.axis_index("ctx")
    x, y = place // 32, place % NY
    moves = list(zip(others, refs[n + more + 1 : -1]))
    for i, (dx, dy) in enumerate(PLANE):
        slot = (x + dx) % NX * NY + (y + dy) % NY
        moves.append((pieces[i], out.at[pl.ds(pl.multiple_of(slot * RB, RB), RB)]))
    copies = []
    for i, (source, target) in enumerate(moves):
        copies.append(pltpu.make_async_copy(source, target, sem.at[i]))
        copies[-1].start()
    for c in copies:
        c.wait()


def plane(pieces, *others):
    n = len(pieces)
    return pl.pallas_call(
        plane_kernel,
        out_shape=(jax.ShapeDtypeStruct((n * RB, 2 * DH), jnp.bfloat16),)
        + tuple(jax.ShapeDtypeStruct(a.shape, a.dtype) for a in others),
        in_specs=[pl.BlockSpec(memory_space=pl.ANY)] * (n + len(others)),
        out_specs=(pl.BlockSpec(memory_space=pltpu.VMEM),) * (1 + len(others)),
        scratch_shapes=[pltpu.SemaphoreType.DMA((n + len(others),))],
        compiler_params=SMALL,
        name="plane",
    )(*pieces, *others)


def local(queries, keys, values, steal_block):
    sent_a, sent_b = pack(keys, values)
    sent_q, kept = part(steal_block, queries)

    def send(array, dx, dz, dy):
        return lax.ppermute(array, "ctx", shift(dx, dz, dy))

    def step(units, state, last=False):
        return absorb(units, steal_block, state, last)

    kv_a = lax.all_to_all(sent_a, "ctx", 0, 0, axis_index_groups=Z_LINES, tiled=True)
    b = {(0, 0): sent_b}
    b[1, 0] = send(sent_b, 1, 0, 0)
    b[0, 1] = send(sent_b, 0, 0, -1)
    b[0, 3] = send(sent_b, 0, 0, 1)
    b[1, 1] = send(b[0, 1], 1, 0, 0)
    b[0, 2] = send(b[0, 1], 0, 0, -1)
    b[1, 3] = send(b[1, 0], 0, 0, 1)
    b[1, 2] = send(b[0, 2], 1, 0, 0)
    own = lax.ppermute(sent_q, "ctx", MIRROR)
    kv_b, kv_a, kept = plane([b[o] for o in PLANE], kv_a, kept)

    xa = send(kv_a, 1, 0, 0)
    yp = send(kv_a, 0, 0, -1)
    ym = send(kv_a, 0, 0, 1)
    xyp = send(yp, 1, 0, 0)
    y2 = send(yp, 0, 0, -1)
    xym = send(xa, 0, 0, 1)
    xy2 = send(y2, 1, 0, 0)

    ring = {0: kv_b}
    for d in (1, 2, 3):
        ring[d] = send(ring[d - 1], 0, -1, 0)
        ring[-d] = send(ring[1 - d], 0, 1, 0)
    ring[4] = send(ring[3], 0, -1, 0)

    def far(*ds):
        return [("b", ring[d], (0, d, 0)) for d in ds]

    state = step([("a", kv_a, (0, 0, 0)), *far(0)], (own, kept))
    near = [("a", xa, (1, 0, 0)), ("a", yp, (0, 0, 1)), ("a", ym, (0, 0, -1))]
    state = step([*near, *far(1, -1)], state)
    after = [("a", xyp, (1, 0, 1)), ("a", y2, (0, 0, 2)), ("a", xym, (1, 0, -1))]
    state = step([*after, *far(2, -2)], state)
    state = step(far(3, -3, 4), state)
    return step([("a", xy2, (1, 0, 2))], state, last=True)


def solution(mesh):
    placed = (P(("batch", "ctx"), None), P(("batch", "ctx"), None), P(("batch", "ctx"), None), P())
    return jax.shard_map(
        local, mesh=mesh, in_specs=placed, out_specs=P(("batch", "ctx"), None), check_vma=False
    )
```

```python
import functools

import jax
import jax.numpy as jnp
import numpy as np
from jax import lax
from jax.experimental import pallas as pl
from jax.experimental.pallas import tpu as pltpu
from jax.sharding import PartitionSpec as P

NX, NZ, NY = 2, 8, 4
TOK = 192
BLK = 96
HEADS, DH = 8, 128
ROWS = BLK * HEADS
RA, RB = 128, 64
TILE = 256
GROUP = 8
MAX_TILES = 24
SMALL = pltpu.CompilerParams(vmem_limit_bytes=6 * 1024 * 1024)
NOWHERE = 1 << 20
COST = 8
HT = 4
RT = BLK * HT
SCALE = float(np.log2(np.e) / np.sqrt(DH))
UNSEEN = -1e30
NO_MAX = -1e20


def dev(x, z, y):
    return (x % NX) * 32 + (z % NZ) * 4 + (y % NY)


def shift(dx, dz, dy):
    return [
        (dev(x, z, y), dev(x + dx, z + dz, y + dy))
        for x in range(NX)
        for z in range(NZ)
        for y in range(NY)
    ]


Z_LINES = [[dev(x, z, y) for z in range(NZ)] for x in range(NX) for y in range(NY)]
XY_PLANES = [[dev(x, z, y) for x in range(NX) for y in range(NY)] for z in range(NZ)]
PLANE = [(dx, dy) for dx in range(NX) for dy in range(NY)]
MIRROR = [(d, 63 - d) for d in range(64)]

def tile_base(kind, t, base):
    return base + t * (2 * 768 if kind == "a" else 32 * TOK)


def whereabouts(steal_ref):
    place = lax.axis_index("ctx")
    return place, steal_ref[jnp.minimum(place, 63 - place)]


def kernel(kinds, bases, cuts, first, last, *refs):
    n = sum(cuts)
    steal_ref = refs[0]
    units, refs = refs[1 : 1 + n], refs[1 + n :]
    if first:
        own_ref, kept_ref, q_ref = refs[0], refs[1], refs[2]
        refs = refs[3:]
    else:
        q_ref, m_in, l_in, acc_in = refs[:4]
        refs = refs[4:]
    if last:
        out = refs[0]
        refs = refs[1:]
    m_ref, l_ref, acc_ref, kv_ref, pos_ref, low_ref, kind_ref, list_ref = refs[:8]
    tiles = []
    for u, kind in enumerate(kinds):
        count = (NZ * RA if kind == "a" else NX * NY * RB) // TILE
        size = count * TILE // cuts[u]
        for i in range(cuts[u]):
            at = len(tiles) * TILE + i * size
            kv_ref[pl.ds(at, size), :] = units[sum(cuts[:u]) + i][...]
        tiles += [(u, kind, t) for t in range(count)]
    place, traded = whereabouts(steal_ref)
    if first:
        m_ref[...] = jnp.full(m_ref.shape, NO_MAX, jnp.float32)
        l_ref[...] = jnp.zeros(l_ref.shape, jnp.float32)
        acc_ref[...] = jnp.zeros(acc_ref.shape, jnp.float32)
    elif last:
        m_ref[...] = m_in[...]
        l_ref[...] = l_in[...]
        acc_ref[...] = acc_in[...]
    key = lax.broadcasted_iota(jnp.int32, (1, TILE), 1)
    pos_ref[0:1, :] = key + key // RA * (NY * TOK - RA)
    pos_ref[1:2, :] = key + key // RB * (TOK - RB)
    x, z, y = place // 32, (place // NY) % NZ, place % NY
    starts = ((63 - place) * TOK + traded * BLK, place * TOK + (1 - traded) * BLK)
    total = len(tiles)
    counts = [0, 0]
    low_ref[total] = NOWHERE
    kind_ref[total] = 0
    for i, (u, kind, t) in enumerate(tiles):
        dx, dz, dy = bases[u]
        if kind == "a":
            base = ((x + dx) % NX * 32 + (y + dy + NY) % NY) * TOK
        else:
            base = (z + dz + NZ) % NZ * NY * TOK + RA
        low = tile_base(kind, t, base)
        low_ref[i] = low
        kind_ref[i] = 0 if kind == "a" else 1
        for b in range(2):
            list_ref[b * (MAX_TILES + 1) + counts[b]] = i
            counts[b] = counts[b] + jnp.where(low <= starts[b] + (BLK - 1), 1, 0)
    for b in range(2):
        list_ref[b * (MAX_TILES + 1) + counts[b]] = total
        counts[b] = counts[b] + jnp.where(counts[b] % 4 == 3, 1, 0)
    if first:
        for b, ref in enumerate((own_ref, kept_ref)):
            for h in range(HEADS):
                q_ref[pl.ds(b * ROWS + h * BLK, BLK), :] = ref[:, h * DH : (h + 1) * DH]

    def block(b, _):
        start = jnp.where(b == 0, starts[0], starts[1])
        count = jnp.where(b == 0, counts[0], counts[1])

        def group(at, size):
            index = [list_ref[b * (MAX_TILES + 1) + at + j] for j in range(size)]
            here = [pl.ds(pl.multiple_of(jnp.minimum(i, total - 1) * TILE, TILE), TILE) for i in index]
            k = jnp.concatenate([kv_ref[r, :DH] for r in here], axis=0)
            v = jnp.concatenate([kv_ref[r, DH:] for r in here], axis=0)
            kpos = jnp.concatenate([pos_ref[pl.ds(kind_ref[i], 1), :] + low_ref[i] for i in index], axis=1)
            qpos = start + lax.broadcasted_iota(jnp.int32, (BLK, size * TILE), 0)
            bias = jnp.where(kpos <= qpos, 0.0, UNSEEN)
            bias = jnp.concatenate([bias] * HT, axis=0)
            lanes = size * TILE // 128

            def rows(r):
                return pl.ds(pl.multiple_of(b * ROWS + r * RT, RT), RT)

            def score(r):
                q = q_ref[rows(r), :]
                return lax.dot_general(q, k, (((1,), (1,)), ((), ())), preferred_element_type=jnp.float32)

            def weigh(r, s):
                s = s + bias
                old = m_ref[rows(r), :]
                m = functools.reduce(jnp.maximum, [s[:, i * 128 : (i + 1) * 128] for i in range(lanes)])
                m = jnp.maximum(old, jnp.broadcast_to(jnp.max(m, axis=1, keepdims=True), (RT, 128)))
                m_ref[rows(r), :] = m
                alpha = jnp.exp2((old - m) * SCALE)
                p = jnp.exp2(s * SCALE - jnp.concatenate([m * SCALE] * lanes, axis=1))
                part = functools.reduce(jnp.add, [p[:, i * 128 : (i + 1) * 128] for i in range(lanes)])
                l_ref[rows(r), :] = l_ref[rows(r), :] * alpha + part
                return p.astype(jnp.bfloat16), alpha

            def add(r, p, alpha):
                acc_ref[rows(r), :] = acc_ref[rows(r), :] * alpha + jnp.dot(p, v, preferred_element_type=jnp.float32)

            steps = HEADS // HT
            s = score(0)
            done = None
            for r in range(steps):
                after = score(r + 1) if r + 1 < steps else None
                weighed = weigh(r, s)
                if done is not None:
                    add(r - 1, *done)
                done, s = weighed, after
            add(steps - 1, *done)

        def whole(g, _):
            group(g * GROUP, GROUP)
            return 0

        lax.fori_loop(0, count // GROUP, whole, 0)
        size = GROUP // 2
        while size:

            @pl.when(count // size % 2 == 1)
            def _(size=size):
                group(count // (2 * size) * (2 * size), size)

            size //= 2

        if last:
            row = pl.multiple_of(jnp.where(b == 0, traded, 1 - traded) * BLK, 32)
            for h in range(HEADS):
                at = pl.ds(pl.multiple_of(b * ROWS + h * BLK, BLK), BLK)
                ctx = acc_ref[at, :] / jnp.sum(l_ref[at, :], axis=1, keepdims=True)
                out[pl.ds(row, BLK), h * DH : (h + 1) * DH] = ctx.astype(jnp.bfloat16)
        return 0

    lax.fori_loop(0, 2, block, 0)


def absorb(units, steal_block, state, last=False):
    kinds = tuple(k for k, _, _ in units)
    bases = tuple(o for _, _, o in units)
    arrays = [a if isinstance(a, tuple) else (a,) for _, a, _ in units]
    cuts = tuple(len(a) for a in arrays)
    first = len(state) == 2
    vmem = pl.BlockSpec(memory_space=pltpu.VMEM)
    ops = [steal_block] + [p for a in arrays for p in a] + list(state)
    shape = jax.ShapeDtypeStruct((2 * ROWS, DH), jnp.float32)
    keys = sum(NZ * RA if k == "a" else NX * NY * RB for k in kinds)
    count = keys // TILE
    scratch = [
        pltpu.VMEM((keys, 2 * DH), jnp.bfloat16),
        pltpu.VMEM((8, TILE), jnp.int32),
        pltpu.SMEM((count + 1,), jnp.int32),
        pltpu.SMEM((count + 1,), jnp.int32),
        pltpu.SMEM((2 * (MAX_TILES + 1),), jnp.int32),
    ]
    aliases = {}
    if last:
        out_shape = jax.ShapeDtypeStruct((TOK, HEADS * DH), jnp.bfloat16)
        out_specs = vmem
        scratch = [pltpu.VMEM(shape.shape, jnp.float32)] * 3 + scratch
    else:
        out_shape, out_specs = (shape,) * 3, (vmem,) * 3
        if first:
            out_shape = (jax.ShapeDtypeStruct((2 * ROWS, DH), jnp.bfloat16),) + out_shape
            out_specs = (vmem,) * 4
        else:
            aliases = {len(ops) - 3 + i: i for i in range(3)}
    got = pl.pallas_call(
        functools.partial(kernel, kinds, bases, cuts, first, last),
        out_shape=out_shape,
        in_specs=[pl.BlockSpec(memory_space=pltpu.SMEM)]
        + [vmem] * (len(ops) - 1),
        out_specs=out_specs,
        scratch_shapes=scratch,
        input_output_aliases=aliases,
        compiler_params=pltpu.CompilerParams(vmem_limit_bytes=24 * 1024 * 1024),
        cost_estimate=pl.CostEstimate(
            flops=COST * 2 * ROWS * keys * DH * 2, bytes_accessed=4 << 20, transcendentals=ROWS * keys
        ),
        name="absorb",
    )(*ops)
    return got if first or last else (state[0], *got)


def pack_kernel(keys_ref, values_ref, a_ref, b_ref):
    for i in range(NZ):
        a_ref[pl.ds(i * RA, RA), :DH] = keys_ref[:RA, :]
        a_ref[pl.ds(i * RA, RA), DH:] = values_ref[:RA, :]
    b_ref[:, :DH] = keys_ref[RA:, :]
    b_ref[:, DH:] = values_ref[RA:, :]


def pack(keys, values):
    vmem = pl.BlockSpec(memory_space=pltpu.VMEM)
    return pl.pallas_call(
        pack_kernel,
        out_shape=(
            jax.ShapeDtypeStruct((NZ * RA, 2 * DH), jnp.bfloat16),
            jax.ShapeDtypeStruct((RB, 2 * DH), jnp.bfloat16),
        ),
        in_specs=[vmem] * 2,
        out_specs=(vmem,) * 2,
        name="pack",
    )(keys, values)


def part_kernel(steal_ref, queries_ref, own_ref, kept_ref, sem):
    _, traded = whereabouts(steal_ref)
    copies = []
    for i, (ref, b) in enumerate(((own_ref, traded), (kept_ref, 1 - traded))):
        rows = pl.ds(pl.multiple_of(b * BLK, 32), BLK)
        copies.append(pltpu.make_async_copy(queries_ref.at[rows], ref, sem.at[i]))
        copies[-1].start()
    for c in copies:
        c.wait()


def part(steal_block, queries):
    vmem = pl.BlockSpec(memory_space=pltpu.VMEM)
    return pl.pallas_call(
        part_kernel,
        out_shape=(jax.ShapeDtypeStruct((BLK, HEADS * DH), jnp.bfloat16),) * 2,
        in_specs=[pl.BlockSpec(memory_space=pltpu.SMEM), pl.BlockSpec(memory_space=pl.ANY)],
        out_specs=(vmem,) * 2,
        scratch_shapes=[pltpu.SemaphoreType.DMA((2,))],
        compiler_params=SMALL,
        name="part",
    )(steal_block, queries)


def plane_kernel(*refs):
    n, more = NX * NY, (len(refs) - NX * NY - 2) // 2
    pieces, others, out, sem = refs[:n], refs[n : n + more], refs[n + more], refs[-1]
    place = lax.axis_index("ctx")
    x, y = place // 32, place % NY
    moves = list(zip(others, refs[n + more + 1 : -1]))
    for i, (dx, dy) in enumerate(PLANE):
        slot = (x + dx) % NX * NY + (y + dy) % NY
        moves.append((pieces[i], out.at[pl.ds(pl.multiple_of(slot * RB, RB), RB)]))
    copies = []
    for i, (source, target) in enumerate(moves):
        copies.append(pltpu.make_async_copy(source, target, sem.at[i]))
        copies[-1].start()
    for c in copies:
        c.wait()


def plane(pieces, *others):
    n = len(pieces)
    return pl.pallas_call(
        plane_kernel,
        out_shape=(jax.ShapeDtypeStruct((n * RB, 2 * DH), jnp.bfloat16),)
        + tuple(jax.ShapeDtypeStruct(a.shape, a.dtype) for a in others),
        in_specs=[pl.BlockSpec(memory_space=pl.ANY)] * (n + len(others)),
        out_specs=(pl.BlockSpec(memory_space=pltpu.VMEM),) * (1 + len(others)),
        scratch_shapes=[pltpu.SemaphoreType.DMA((n + len(others),))],
        compiler_params=SMALL,
        name="plane",
    )(*pieces, *others)


def local(queries, keys, values, steal_block):
    sent_a, sent_b = pack(keys, values)
    sent_q, kept = part(steal_block, queries)

    def send(array, dx, dz, dy):
        return lax.ppermute(array, "ctx", shift(dx, dz, dy))

    def step(units, state, last=False):
        return absorb(units, steal_block, state, last)

    kv_a = lax.all_to_all(sent_a, "ctx", 0, 0, axis_index_groups=Z_LINES, tiled=True)
    b = {(0, 0): sent_b}
    b[1, 0] = send(sent_b, 1, 0, 0)
    b[0, 1] = send(sent_b, 0, 0, -1)
    b[0, 3] = send(sent_b, 0, 0, 1)
    b[1, 1] = send(b[0, 1], 1, 0, 0)
    b[0, 2] = send(b[0, 1], 0, 0, -1)
    b[1, 3] = send(b[1, 0], 0, 0, 1)
    b[1, 2] = send(b[0, 2], 1, 0, 0)
    own = lax.ppermute(sent_q, "ctx", MIRROR)
    kv_b, kv_a, kept = plane([b[o] for o in PLANE], kv_a, kept)

    xa = send(kv_a, 1, 0, 0)
    yp = send(kv_a, 0, 0, -1)
    ym = send(kv_a, 0, 0, 1)
    xyp = send(yp, 1, 0, 0)
    y2 = send(yp, 0, 0, -1)
    xym = send(xa, 0, 0, 1)
    half = NZ * RA // 2
    xy2 = (send(xyp[:half], 0, 0, -1), send(xym[half:], 0, 0, 1))

    ring = {0: kv_b}
    for d in (1, 2, 3):
        ring[d] = send(ring[d - 1], 0, -1, 0)
        ring[-d] = send(ring[1 - d], 0, 1, 0)
    ring[4] = send(ring[3], 0, -1, 0)

    def far(*ds):
        return [("b", ring[d], (0, d, 0)) for d in ds]

    near = [("a", kv_a, (0, 0, 0)), ("a", xa, (1, 0, 0)), ("a", yp, (0, 0, 1)), ("a", ym, (0, 0, -1))]
    state = step([*near, *far(0, 1, -1)], (own, kept))
    after = [("a", xyp, (1, 0, 1)), ("a", y2, (0, 0, 2)), ("a", xym, (1, 0, -1))]
    state = step([*after, *far(2, -2, 3, -3)], state)
    return step([("a", xy2, (1, 0, 2)), *far(4)], state, last=True)


def solution(mesh):
    placed = (P(("batch", "ctx"), None), P(("batch", "ctx"), None), P(("batch", "ctx"), None), P())
    return jax.shard_map(
        local, mesh=mesh, in_specs=placed, out_specs=P(("batch", "ctx"), None), check_vma=False
    )
```
